32 devices in a mesh: dp: 2 (over x), fsdp: 2 (over core), tensor: 8 (over z, y).
Axes of the slice: x: 2, y: 2, z: 4, core: 2. Of those that a mesh axis runs over, the one named last changes fastest.
Arguments:
- weight: float32 [4096, 8192], P('fsdp', 'tensor'), may hold values from -6 to 6
- momentum: float32 [4096, 8192], P('fsdp', 'tensor'), may hold values from -180 to 180
- right_basis: float32 [256, 8192], P('fsdp', 'tensor'), may hold values from -0.0625 to 0.0625
- gradients: bfloat16 [1, 2, 4096, 8192], P(None, 'dp', 'fsdp', 'tensor'), may hold values from -6 to 6
Outputs:
- new_weight: float32 [4096, 8192], P('fsdp', 'tensor')
- new_momentum: float32 [4096, 8192], P('fsdp', 'tensor')
- new_basis: float32 [256, 8192], P('fsdp', 'tensor')
The draws below stay inside these ranges and needn't reach their ends.
All inputs are finite; a program needn't handle non-finite values.
Results may differ from the reference program's by a relative error of at most 0.0003.
Values sent between devices are 32-bit elements; how exact they have to be, the bound alone decides.
A program may use at most 128 MiB of HBM per device.

```python
import math
import jax
import jax.numpy as jnp
from jax import lax

D = 8192
ROWS = 4096
RANK = 256
STEPS = 1
N_DP = 2


def draw_momentum(key, part):
    base_key, col_key, row_key = jax.random.split(jax.random.fold_in(key, 11), 3)
    column_ramp = jnp.arange(D, dtype=jnp.float32) / D
    col_scale = jnp.exp(math.log(3.0) * column_ramp + jax.random.uniform(col_key, (D,), jnp.float32, 0.0, math.log(10.0)))
    row_scale = jnp.exp(jax.random.uniform(row_key, (ROWS, 1), jnp.float32, 0.0, math.log(4.0)))
    values = jnp.clip(jax.random.normal(base_key, (ROWS, D), jnp.float32), -6.0, 6.0)
    return 0.25 * values * row_scale * col_scale[None, :]


def steps_of(own_key, dims, cuts, least, top_value):
    loudness, own = 1.0, jax.random.fold_in(own_key, 6)
    for position, blocks in cuts:
        heights = jnp.exp(jax.random.uniform(jax.random.fold_in(own, position), (blocks,), jnp.float32, least / len(cuts), top_value / len(cuts)))
        loudness = loudness * jnp.repeat(heights, dims[position] // blocks).reshape([-1 if axis == position else 1 for axis in range(len(dims))])
    return loudness


def normal_values(stream_key, extent, spread, bound, cuts=(), held_as=jnp.bfloat16):
    gain = steps_of(stream_key, extent, cuts, -0.22, 0.18) if cuts else 1.0
    array = jax.random.normal(stream_key, extent, jnp.float32) * spread * gain
    return jnp.minimum(jnp.maximum(array, -bound), bound).astype(held_as)


def setup_inputs(seed: int = 0) -> dict:
    splits = jax.random.split(jax.random.key(seed), 5)
    return {
        "weight": normal_values(splits[0], (ROWS, D), 1.0, 6.0, ((0, 2), (1, 8)), jnp.float32),
        "momentum": draw_momentum(jax.random.fold_in(splits[4], 71), 0),
        "right_basis": normal_values(splits[2], (RANK, D), D ** -0.5, 0.0625, ((0, 2), (1, 8)), jnp.float32),
        "gradients": normal_values(splits[3], (STEPS, N_DP, ROWS, D), 1.0, 6.0, ((1, 2), (2, 2), (3, 8))),
    }


highest = lax.Precision.HIGHEST
step_size = 0.3
drop_share = 0.05
guard_term = 1e-06

def contract(left, right, left_dim, right_dim):
    return lax.dot_general(left.astype(jnp.float32), right.astype(jnp.float32), (((left_dim,), (right_dim,)), ((), ())), precision=highest, preferred_element_type=jnp.float32)

def orthonormal(sketch):
    gram_matrix = contract(sketch, sketch, 0, 0)
    lower_factor = jnp.linalg.cholesky(gram_matrix)
    return lax.linalg.triangular_solve(lower_factor, sketch, left_side=False, lower=True, transpose_a=True)

def reference(weight, momentum, right_basis, gradients):
    step_scale = step_size * math.sqrt(ROWS * D / RANK)
    for iteration in range(STEPS):
        grad_total = gradients[iteration, 0].astype(jnp.float32)
        for replica in range(1, N_DP):
            grad_total = grad_total + gradients[iteration, replica].astype(jnp.float32)
        momentum = momentum + grad_total
        sketch = contract(momentum, right_basis, 1, 1)
        left_basis = orthonormal(sketch)
        coefficients = contract(left_basis, momentum, 0, 0)
        squares = lax.optimization_barrier(jnp.sum(coefficients * coefficients, axis=1))
        right_basis = coefficients * lax.rsqrt(squares + guard_term)[:, None]
        momentum = momentum - drop_share * contract(left_basis, coefficients, 1, 0)
        weight = weight - step_scale * contract(left_basis, right_basis, 1, 0)
    return (weight, momentum, right_basis)
```

```python
import math

import jax
import jax.numpy as jnp
from jax import lax
from jax.sharding import PartitionSpec as P

highest = lax.Precision.HIGHEST
step_size = 0.3
drop_share = 0.05
guard_term = 1e-06


def contract(left, right, left_dim, right_dim):
    return lax.dot_general(
        left,
        right,
        (((left_dim,), (right_dim,)), ((), ())),
        precision=highest,
        preferred_element_type=jnp.float32,
    )


def inverse_factor(gram):
    lower = jnp.linalg.cholesky(gram)
    eye = jnp.eye(gram.shape[0], dtype=jnp.float32)
    return lax.linalg.triangular_solve(lower, eye, left_side=True, lower=True)


def shards(n_dp, step_scale, weight, momentum, right_basis, gradients):
    share_rows = right_basis.shape[0]
    gradient = gradients[0, 0].astype(jnp.float32)
    other = lax.ppermute(gradient, "dp", [(i, (i + 1) % n_dp) for i in range(n_dp)])
    basis = lax.all_gather(right_basis, "fsdp", axis=0, tiled=True)
    share = momentum * (1.0 / n_dp) + gradient
    part = contract(share, basis, 1, 1)
    block = lax.psum_scatter(part, "tensor", scatter_dimension=0, tiled=True)
    block = lax.psum(block, "dp")
    gram = lax.psum(contract(block, block, 0, 0), ("tensor", "fsdp"))
    sketch = lax.all_gather(block, "tensor", axis=0, tiled=True)
    inverse = inverse_factor(gram)
    product = lax.psum_scatter(contract(sketch, share, 0, 0), "fsdp", scatter_dimension=0, tiled=True)
    product = lax.all_gather(lax.psum(product, "dp"), "fsdp", axis=0, tiled=True)
    coefficients = contract(inverse, product, 1, 0)
    left_basis = contract(sketch, inverse, 1, 1)
    squares = lax.psum(jnp.sum(coefficients * coefficients, axis=1), "tensor")
    scale = lax.rsqrt(squares + guard_term)
    scaled = coefficients * scale[:, None]
    weight = weight - step_scale * contract(left_basis, scaled, 1, 0)
    total = momentum + (gradient + other)
    momentum = total - drop_share * contract(left_basis, coefficients, 1, 0)
    first_rank = lax.axis_index("fsdp") * share_rows
    return weight, momentum, lax.dynamic_slice_in_dim(scaled, first_rank, share_rows, 0)


def solution(mesh):
    n_dp = mesh.shape["dp"]

    def step(weight, momentum, right_basis, gradients):
        rows, width = weight.shape
        step_scale = step_size * math.sqrt(rows * width / right_basis.shape[0])

        def local(*blocks):
            return shards(n_dp, step_scale, *blocks)

        return jax.shard_map(
            local,
            mesh=mesh,
            in_specs=(
                P("fsdp", "tensor"),
                P("fsdp", "tensor"),
                P("fsdp", "tensor"),
                P(None, "dp", "fsdp", "tensor"),
            ),
            out_specs=(P("fsdp", "tensor"), P("fsdp", "tensor"), P("fsdp", "tensor")),
            check_vma=False,
        )(weight, momentum, right_basis, gradients)

    return step
```

```python
import functools
import math

import jax
import jax.numpy as jnp
from jax import lax
from jax.experimental import pallas as pl
from jax.experimental.pallas import tpu as pltpu
from jax.sharding import PartitionSpec as P

highest = lax.Precision.HIGHEST
step_size = 0.3
drop_share = 0.05
guard_term = 1e-06
MESH = pl.DeviceIdType.MESH
PANEL = 32


def contract(left, right, left_dim, right_dim):
    return lax.dot_general(
        left,
        right,
        (((left_dim,), (right_dim,)), ((), ())),
        precision=highest,
        preferred_element_type=jnp.float32,
    )


def factor(aug):
    rank = aug.shape[0]

    @pl.loop(0, rank // PANEL)
    def _(block):
        first = pl.multiple_of(block * PANEL, PANEL)
        row = lax.broadcasted_iota(jnp.int32, (PANEL, 1), 0)
        lane = lax.broadcasted_iota(jnp.int32, (PANEL, rank), 1)

        def eliminate(step, work):
            column = jnp.sum(jnp.where(lane == first + step, work[:, :rank], 0.0), axis=1, keepdims=True)
            pivot = jnp.sum(jnp.where(row == step, column, 0.0), axis=0, keepdims=True)
            root = lax.rsqrt(pivot)
            line = jnp.sum(jnp.where(row == step, work, 0.0), axis=0, keepdims=True) * root
            rest = work - jnp.where(row > step, column * root, 0.0) * line
            return jnp.where(row == step, line, rest)

        work = lax.fori_loop(0, PANEL, eliminate, aug[pl.ds(first, PANEL), :])
        aug[pl.ds(first, PANEL), :] = work
        below = jnp.where(lane >= first + PANEL, work[:, :rank], 0.0)
        aug[...] -= contract(below, work, 0, 0)


def kernel(
    n, momentum, right_basis, gradients, other, left_out, coef_out, scaled_out,
    grad_in, share, grad, basis, part, part_in, own, own_in, sketch,
    gram_part, gram_in, gram_sum, gram_pair, gram_all, aug, left,
    coef_part, coef_in, coef_sum, coef_pair, coef_all, norm_own, norm_in, scale_own, scale_in,
    load_sem, grad_send, grad_recv, pair_send, pair_recv,
    part_send, part_recv, row_send, row_recv, gram_send, gram_recv,
    gall_send, gall_recv, norm_send, norm_recv, base_sem,
):
    dp, core, me = lax.axis_index("dp"), lax.axis_index("fsdp"), lax.axis_index("tensor")
    rows, _ = share.shape
    piece = rows // n
    half = right_basis.shape[0]
    rank = 2 * half
    lines = rank // n

    def at(index):
        return pl.ds(pl.multiple_of(index * piece, piece), piece)

    def load(index, slot):
        return (
            pltpu.make_async_copy(gradients.at[at(index)], grad_in.at[at(index)], load_sem.at[0, slot]),
            pltpu.make_async_copy(momentum.at[at(index)], share.at[at(index)], load_sem.at[1, slot]),
        )

    base = pltpu.make_async_copy(right_basis, basis.at[core], base_sem)
    base.start()

    @pl.loop(0, n)
    def _(k):
        for copy in load(lax.rem(me + k + 1, n), k):
            copy.start()

    barrier = pltpu.get_barrier_semaphore()
    pl.semaphore_signal(barrier, inc=1, device_id={"dp": 1 - dp}, device_id_type=MESH)
    pl.semaphore_signal(barrier, inc=1, device_id={"fsdp": 1 - core}, device_id_type=MESH)

    @pl.loop(1, n)
    def _(k):
        pl.semaphore_signal(barrier, inc=1, device_id={"tensor": lax.rem(me + k, n)}, device_id_type=MESH)

    pl.semaphore_wait(barrier, n + 1)

    def remote(src, dst, send, recv, where):
        return pltpu.make_async_remote_copy(
            src_ref=src, dst_ref=dst, send_sem=send, recv_sem=recv, device_id=where, device_id_type=MESH
        )

    def pair(index, src, dst, axis):
        where = {axis: 1 - (dp if axis == "dp" else core)}
        return remote(src, dst, pair_send.at[index], pair_recv.at[index], where)

    def grad_copy(k):
        index = lax.rem(me + k + 1, n)
        return remote(grad.at[at(index)], other.at[at(index)], grad_send.at[k], grad_recv.at[k], {"dp": 1 - dp})

    def send_grads(begin, end):
        @pl.loop(begin, end)
        def _(k):
            grad_copy(k).start()

    base.wait()
    basis_copy = pair(0, basis.at[core], basis.at[core], "fsdp")
    basis_copy.start()
    stages = [n * i // 8 for i in (3, 5, 6, 7, 8)]

    @pl.loop(0, n)
    def _(k):
        index = lax.rem(me + k + 1, n)
        for copy in load(index, k):
            copy.wait()
        value = grad_in[at(index), :].astype(jnp.float32)
        grad[at(index), :] = value
        share[at(index), :] = share[at(index), :] * 0.5 + value

        @pl.when(k < stages[0])
        def _():
            grad_copy(k).start()

    basis_copy.wait()

    def part_copy(k):
        return remote(
            part.at[lax.rem(me + k, n)], part_in.at[k], part_send.at[k], part_recv.at[k],
            {"tensor": lax.rem(me + k, n)},
        )

    @pl.loop(1, n + 1)
    def _(k):
        index = lax.rem(me + k, n)
        value = share[at(index), :]
        for h in range(2):
            part[index, :, h * half : (h + 1) * half] = contract(value, basis[h], 1, 1)

        @pl.when(k < n)
        def _():
            part_copy(k).start()

    own[...] = part[me]

    @pl.loop(1, n)
    def _(k):
        part_copy(k).wait()
        own[...] += part_in[k]

    dp_copy = pair(1, own, own_in, "dp")
    dp_copy.start()
    send_grads(stages[0], stages[1])
    dp_copy.wait()
    sketch[at(me), :] = own[...] + own_in[...]

    block = sketch[at(me), :]
    gram = contract(block, block, 0, 0)
    for i in range(n):
        gram_part[i] = gram[i * lines : (i + 1) * lines, :]

    def gram_copy(k):
        return remote(
            gram_part.at[lax.rem(me + k, n)], gram_in.at[k], gram_send.at[k], gram_recv.at[k],
            {"tensor": lax.rem(me + k, n)},
        )

    @pl.loop(1, n)
    def _(k):
        gram_copy(k).start()

    gram_sum[...] = gram_part[me]

    @pl.loop(1, n)
    def _(k):
        gram_copy(k).wait()
        gram_sum[...] += gram_in[k]

    gram_swap = pair(2, gram_sum, gram_pair, "fsdp")
    gram_swap.start()
    gram_swap.wait()
    gram_all[me] = gram_sum[...] + gram_pair[...]

    def gall_copy(k):
        return remote(
            gram_all.at[me], gram_all.at[me], gall_send.at[k], gall_recv.at[k], {"tensor": lax.rem(me + k, n)}
        )

    def row_copy(k):
        return remote(
            sketch.at[at(me)], sketch.at[at(me)], row_send.at[k], row_recv.at[k], {"tensor": lax.rem(me + k, n)}
        )

    def gall_arrival(k):
        source = lax.rem(me + n - k, n)
        return remote(
            gram_all.at[source], gram_all.at[source], gall_send.at[k], gall_recv.at[k],
            {"tensor": lax.rem(me + k, n)},
        )

    def row_arrival(k):
        source = lax.rem(me + n - k, n)
        return remote(
            sketch.at[at(source)], sketch.at[at(source)], row_send.at[k], row_recv.at[k],
            {"tensor": lax.rem(me + k, n)},
        )

    @pl.loop(1, n)
    def _(k):
        gall_copy(k).start()

    @pl.loop(1, n)
    def _(k):
        row_copy(k).start()

    send_grads(stages[1], stages[2])

    @pl.loop(1, n)
    def _(k):
        gall_copy(k).wait_send()
        gall_arrival(k).wait_recv()

    for i in range(n):
        aug[i * lines : (i + 1) * lines, :rank] = gram_all[i]
    diagonal = lax.broadcasted_iota(jnp.int32, (rank, rank), 0) == lax.broadcasted_iota(jnp.int32, (rank, rank), 1)
    aug[:, rank:] = jnp.where(diagonal, 1.0, 0.0)
    factor(aug)
    send_grads(stages[2], stages[3])

    @pl.loop(1, n)
    def _(k):
        row_copy(k).wait_send()
        row_arrival(k).wait_recv()

    coef_part[...] = jnp.zeros_like(coef_part)

    @pl.loop(0, n)
    def _(k):
        block = sketch[at(k), :]
        for h in range(2):
            value = contract(block, aug[h * half : (h + 1) * half, rank:], 1, 1)
            left[h, at(k), :] = value
            left_out[at(k), h * half : (h + 1) * half] = value

    def accumulate(h):
        @pl.loop(0, n)
        def _(k):
            coef_part[h] += contract(left[h, at(k), :], share[at(k), :], 0, 0)

    accumulate(1 - core)
    coef_swap = pair(3, coef_part.at[1 - core], coef_in, "fsdp")
    coef_swap.start()
    accumulate(core)
    coef_swap.wait()
    coef_sum[...] = coef_part[core] + coef_in[...]
    coef_dp = pair(4, coef_sum, coef_pair, "dp")
    coef_dp.start()
    send_grads(stages[3], stages[4])
    coef_dp.wait()
    coef_all[core] = coef_sum[...] + coef_pair[...]
    coef_share = pair(5, coef_all.at[core], coef_all.at[core], "fsdp")
    coef_share.start()

    value = coef_all[core]
    norm_own[...] = contract(jnp.ones((8, value.shape[1]), jnp.float32), value * value, 1, 1)

    def norm_copy(k):
        return remote(
            norm_own, norm_in.at[me], norm_send.at[k], norm_recv.at[k], {"tensor": lax.rem(me + k, n)}
        )

    def norm_arrival(k):
        source = lax.rem(me + n - k, n)
        return remote(
            norm_own, norm_in.at[source], norm_send.at[k], norm_recv.at[k], {"tensor": lax.rem(me + k, n)}
        )

    @pl.loop(1, n)
    def _(k):
        norm_copy(k).start()

    norm_in[me] = norm_own[...]

    @pl.loop(1, n)
    def _(k):
        norm_copy(k).wait_send()
        norm_arrival(k).wait_recv()

    total = norm_in[0]
    for i in range(1, n):
        total = total + norm_in[i]
    scale_own[...] = lax.rsqrt(total + guard_term)
    scale_copy = pair(6, scale_own, scale_in, "fsdp")
    scale_copy.start()
    scale_copy.wait()
    coef_share.wait()

    def scaled(h, scale):
        column = jnp.transpose(jnp.broadcast_to(scale[0:1, :], (half, half)))[:, 0:1]
        scaled_out[h] = coef_all[h] * column

    scaled(core, scale_own[...])
    scaled(1 - core, scale_in[...])
    coef_out[...] = coef_all[...]

    @pl.loop(0, n)
    def _(k):
        grad_copy(k).wait()


def exchange(n, momentum, right_basis, gradient):
    rows, cols = momentum.shape
    half = right_basis.shape[0]
    rank = 2 * half
    piece, lines = rows // n, rank // n
    f32 = jnp.float32
    vmem = pltpu.VMEM
    dma = pltpu.SemaphoreType.DMA
    any_spec = pl.BlockSpec(memory_space=pl.ANY)
    vmem_spec = pl.BlockSpec(memory_space=pltpu.VMEM)
    return pl.pallas_call(
        functools.partial(kernel, n),
        out_shape=(
            jax.ShapeDtypeStruct((rows, cols), f32),
            jax.ShapeDtypeStruct((rows, rank), f32),
            jax.ShapeDtypeStruct((2, half, cols), f32),
            jax.ShapeDtypeStruct((2, half, cols), f32),
        ),
        in_specs=[any_spec] * 3,
        out_specs=(any_spec, vmem_spec, vmem_spec, vmem_spec),
        scratch_shapes=[
            vmem((rows, cols), gradient.dtype),
            vmem((rows, cols), f32),
            vmem((rows, cols), f32),
            vmem((2, half, cols), f32),
            vmem((n, piece, rank), f32),
            vmem((n, piece, rank), f32),
            vmem((piece, rank), f32),
            vmem((piece, rank), f32),
            vmem((rows, rank), f32),
            vmem((n, lines, rank), f32),
            vmem((n, lines, rank), f32),
            vmem((lines, rank), f32),
            vmem((lines, rank), f32),
            vmem((n, lines, rank), f32),
            vmem((rank, 2 * rank), f32),
            vmem((2, rows, half), f32),
            vmem((2, half, cols), f32),
            vmem((half, cols), f32),
            vmem((half, cols), f32),
            vmem((half, cols), f32),
            vmem((2, half, cols), f32),
            vmem((8, half), f32),
            vmem((n, 8, half), f32),
            vmem((8, half), f32),
            vmem((8, half), f32),
            dma((2, n)), dma((n,)), dma((n,)), dma((7,)), dma((7,)),
            dma((n,)), dma((n,)), dma((n,)), dma((n,)), dma((n,)), dma((n,)),
            dma((n,)), dma((n,)), dma((n,)), dma((n,)), dma,
        ],
        compiler_params=pltpu.CompilerParams(
            collective_id=0, has_side_effects=True, vmem_limit_bytes=56 * 1024 * 1024
        ),
        cost_estimate=pl.CostEstimate(
            flops=6 * rows * cols * rank, bytes_accessed=20 * rows * cols, transcendentals=0
        ),
    )(momentum, right_basis, gradient)


def shards(n, step_scale, weight, momentum, right_basis, gradients):
    half, cols = right_basis.shape
    gradient = gradients[0, 0]
    other, left_basis, coefficients, scaled = exchange(n, momentum, right_basis, gradient)
    flat = scaled.reshape(2 * half, cols)
    weight = weight - step_scale * contract(left_basis, flat, 1, 0)
    total = momentum + (gradient.astype(jnp.float32) + other)
    momentum = total - drop_share * contract(left_basis, coefficients.reshape(2 * half, cols), 1, 0)
    first_rank = lax.axis_index("fsdp") * half
    return weight, momentum, lax.dynamic_slice_in_dim(flat, first_rank, half, 0)


def solution(mesh):
    assert mesh.shape["dp"] == 2 and mesh.shape["fsdp"] == 2
    n = mesh.shape["tensor"]

    def step(weight, momentum, right_basis, gradients):
        rows, width = weight.shape
        step_scale = step_size * math.sqrt(rows * width / right_basis.shape[0])
        return jax.shard_map(
            functools.partial(shards, n, step_scale),
            mesh=mesh,
            in_specs=(
                P("fsdp", "tensor"),
                P("fsdp", "tensor"),
                P("fsdp", "tensor"),
                P(None, "dp", "fsdp", "tensor"),
            ),
            out_specs=(P("fsdp", "tensor"), P("fsdp", "tensor"), P("fsdp", "tensor")),
            check_vma=False,
        )(weight, momentum, right_basis, gradients)

    return step
```

```python
import functools
import math

import jax
import jax.numpy as jnp
from jax import lax
from jax.experimental import pallas as pl
from jax.experimental.pallas import tpu as pltpu
from jax.sharding import PartitionSpec as P

highest = lax.Precision.HIGHEST
step_size = 0.3
drop_share = 0.05
guard_term = 1e-06
MESH = pl.DeviceIdType.MESH
PANEL = 32


def contract(left, right, left_dim, right_dim):
    return lax.dot_general(
        left,
        right,
        (((left_dim,), (right_dim,)), ((), ())),
        precision=highest,
        preferred_element_type=jnp.float32,
    )


def factor(aug):
    rank = aug.shape[0]

    @pl.loop(0, rank // PANEL)
    def _(block):
        first = pl.multiple_of(block * PANEL, PANEL)
        row = lax.broadcasted_iota(jnp.int32, (PANEL, 1), 0)
        lane = lax.broadcasted_iota(jnp.int32, (PANEL, rank), 1)

        def eliminate(step, work):
            column = jnp.sum(jnp.where(lane == first + step, work[:, :rank], 0.0), axis=1, keepdims=True)
            pivot = jnp.sum(jnp.where(row == step, column, 0.0), axis=0, keepdims=True)
            root = lax.rsqrt(pivot)
            line = jnp.sum(jnp.where(row == step, work, 0.0), axis=0, keepdims=True) * root
            rest = work - jnp.where(row > step, column * root, 0.0) * line
            return jnp.where(row == step, line, rest)

        work = lax.fori_loop(0, PANEL, eliminate, aug[pl.ds(first, PANEL), :])
        aug[pl.ds(first, PANEL), :] = work
        below = jnp.where(lane >= first + PANEL, work[:, :rank], 0.0)
        aug[...] -= contract(below, work, 0, 0)


def kernel(
    n, momentum, right_basis, gradients, total_out, left_out, coef_out, scaled_out,
    grad_in, share, grad, other, basis, part, part_in, own, own_in, sketch,
    gram_part, gram_in, gram_sum, gram_pair, gram_all, aug, left,
    coef_part, coef_in, coef_sum, coef_pair, coef_all, norm_own, norm_in, scale_own, scale_in,
    load_sem, grad_send, grad_recv, pair_send, pair_recv,
    part_send, part_recv, row_send, row_recv, gram_send, gram_recv,
    gall_send, gall_recv, norm_send, norm_recv, total_sem, base_sem,
):
    dp, core, me = lax.axis_index("dp"), lax.axis_index("fsdp"), lax.axis_index("tensor")
    rows, _ = share.shape
    piece = rows // n
    half = right_basis.shape[0]
    rank = 2 * half
    lines = rank // n

    def at(index):
        return pl.ds(pl.multiple_of(index * piece, piece), piece)

    def load_momentum(index, slot):
        return pltpu.make_async_copy(momentum.at[at(index)], share.at[at(index)], load_sem.at[1, slot])

    def load(index, slot):
        return (
            pltpu.make_async_copy(gradients.at[at(index)], grad_in.at[at(index)], load_sem.at[0, slot]),
            load_momentum(index, slot),
        )

    base = pltpu.make_async_copy(right_basis, basis.at[core], base_sem)
    base.start()

    @pl.loop(0, n)
    def _(k):
        for copy in load(lax.rem(me + k + 1, n), k):
            copy.start()

    barrier = pltpu.get_barrier_semaphore()
    pl.semaphore_signal(barrier, inc=1, device_id={"dp": 1 - dp}, device_id_type=MESH)
    pl.semaphore_signal(barrier, inc=1, device_id={"fsdp": 1 - core}, device_id_type=MESH)

    @pl.loop(1, n)
    def _(k):
        pl.semaphore_signal(barrier, inc=1, device_id={"tensor": lax.rem(me + k, n)}, device_id_type=MESH)

    pl.semaphore_wait(barrier, n + 1)

    def remote(src, dst, send, recv, where):
        return pltpu.make_async_remote_copy(
            src_ref=src, dst_ref=dst, send_sem=send, recv_sem=recv, device_id=where, device_id_type=MESH
        )

    def pair(index, src, dst, axis):
        where = {axis: 1 - (dp if axis == "dp" else core)}
        return remote(src, dst, pair_send.at[index], pair_recv.at[index], where)

    def grad_copy(k):
        index = lax.rem(me + k + 1, n)
        return remote(grad.at[at(index)], other.at[at(index)], grad_send.at[k], grad_recv.at[k], {"dp": 1 - dp})

    def send_grads(begin, end):
        @pl.loop(begin, end)
        def _(k):
            grad_copy(k).start()

    base.wait()
    basis_copy = pair(0, basis.at[core], basis.at[core], "fsdp")
    basis_copy.start()
    stages = [n * i // 8 for i in (4, 6, 7, 8, 8)]

    @pl.loop(0, n)
    def _(k):
        index = lax.rem(me + k + 1, n)
        for copy in load(index, k):
            copy.wait()
        value = grad_in[at(index), :].astype(jnp.float32)
        grad[at(index), :] = value
        share[at(index), :] = share[at(index), :] * 0.5 + value

        @pl.when(k < stages[0])
        def _():
            grad_copy(k).start()

    basis_copy.wait()

    def part_copy(k):
        return remote(
            part.at[lax.rem(me + k, n)], part_in.at[k], part_send.at[k], part_recv.at[k],
            {"tensor": lax.rem(me + k, n)},
        )

    @pl.loop(1, n + 1)
    def _(k):
        index = lax.rem(me + k, n)
        value = share[at(index), :]
        for h in range(2):
            part[index, :, h * half : (h + 1) * half] = contract(value, basis[h], 1, 1)

        @pl.when(k < n)
        def _():
            part_copy(k).start()

    own[...] = part[me]

    @pl.loop(1, n)
    def _(k):
        part_copy(k).wait()
        own[...] += part_in[k]

    dp_copy = pair(1, own, own_in, "dp")
    dp_copy.start()
    send_grads(stages[0], stages[1])
    dp_copy.wait()
    sketch[at(me), :] = own[...] + own_in[...]

    block = sketch[at(me), :]
    gram = contract(block, block, 0, 0)
    for i in range(n):
        gram_part[i] = gram[i * lines : (i + 1) * lines, :]

    def gram_copy(k):
        return remote(
            gram_part.at[lax.rem(me + k, n)], gram_in.at[k], gram_send.at[k], gram_recv.at[k],
            {"tensor": lax.rem(me + k, n)},
        )

    @pl.loop(1, n)
    def _(k):
        gram_copy(k).start()

    gram_sum[...] = gram_part[me]

    @pl.loop(1, n)
    def _(k):
        gram_copy(k).wait()
        gram_sum[...] += gram_in[k]

    gram_swap = pair(2, gram_sum, gram_pair, "fsdp")
    gram_swap.start()
    gram_swap.wait()
    gram_all[me] = gram_sum[...] + gram_pair[...]

    def gall_copy(k):
        return remote(
            gram_all.at[me], gram_all.at[me], gall_send.at[k], gall_recv.at[k], {"tensor": lax.rem(me + k, n)}
        )

    def row_copy(k):
        return remote(
            sketch.at[at(me)], sketch.at[at(me)], row_send.at[k], row_recv.at[k], {"tensor": lax.rem(me + k, n)}
        )

    def gall_arrival(k):
        source = lax.rem(me + n - k, n)
        return remote(
            gram_all.at[source], gram_all.at[source], gall_send.at[k], gall_recv.at[k],
            {"tensor": lax.rem(me + k, n)},
        )

    def row_arrival(k):
        source = lax.rem(me + n - k, n)
        return remote(
            sketch.at[at(source)], sketch.at[at(source)], row_send.at[k], row_recv.at[k],
            {"tensor": lax.rem(me + k, n)},
        )

    @pl.loop(1, n)
    def _(k):
        gall_copy(k).start()

    @pl.loop(1, n)
    def _(k):
        row_copy(k).start()

    send_grads(stages[1], stages[2])

    @pl.loop(1, n)
    def _(k):
        gall_copy(k).wait_send()
        gall_arrival(k).wait_recv()

    for i in range(n):
        aug[i * lines : (i + 1) * lines, :rank] = gram_all[i]
    diagonal = lax.broadcasted_iota(jnp.int32, (rank, rank), 0) == lax.broadcasted_iota(jnp.int32, (rank, rank), 1)
    aug[:, rank:] = jnp.where(diagonal, 1.0, 0.0)
    factor(aug)
    send_grads(stages[2], stages[3])

    @pl.loop(1, n)
    def _(k):
        row_copy(k).wait_send()
        row_arrival(k).wait_recv()

    coef_part[...] = jnp.zeros_like(coef_part)

    @pl.loop(0, n)
    def _(k):
        block = sketch[at(k), :]
        for h in range(2):
            value = contract(block, aug[h * half : (h + 1) * half, rank:], 1, 1)
            left[h, at(k), :] = value
            left_out[at(k), h * half : (h + 1) * half] = value

    def accumulate(h):
        @pl.loop(0, n)
        def _(k):
            coef_part[h] += contract(left[h, at(k), :], share[at(k), :], 0, 0)

    accumulate(1 - core)
    coef_swap = pair(3, coef_part.at[1 - core], coef_in, "fsdp")
    coef_swap.start()
    accumulate(core)

    @pl.loop(0, n)
    def _(k):
        load_momentum(lax.rem(me + k + 1, n), k).start()

    coef_swap.wait()
    coef_sum[...] = coef_part[core] + coef_in[...]
    coef_dp = pair(4, coef_sum, coef_pair, "dp")
    coef_dp.start()
    send_grads(stages[3], stages[4])
    coef_dp.wait()
    coef_all[core] = coef_sum[...] + coef_pair[...]
    coef_share = pair(5, coef_all.at[core], coef_all.at[core], "fsdp")
    coef_share.start()

    value = coef_all[core]
    norm_own[...] = contract(jnp.ones((8, value.shape[1]), jnp.float32), value * value, 1, 1)

    def norm_copy(k):
        return remote(
            norm_own, norm_in.at[me], norm_send.at[k], norm_recv.at[k], {"tensor": lax.rem(me + k, n)}
        )

    def norm_arrival(k):
        source = lax.rem(me + n - k, n)
        return remote(
            norm_own, norm_in.at[source], norm_send.at[k], norm_recv.at[k], {"tensor": lax.rem(me + k, n)}
        )

    @pl.loop(1, n)
    def _(k):
        norm_copy(k).start()

    norm_in[me] = norm_own[...]

    @pl.loop(1, n)
    def _(k):
        norm_copy(k).wait_send()
        norm_arrival(k).wait_recv()

    total = norm_in[0]
    for i in range(1, n):
        total = total + norm_in[i]
    scale_own[...] = lax.rsqrt(total + guard_term)
    scale_copy = pair(6, scale_own, scale_in, "fsdp")
    scale_copy.start()
    scale_copy.wait()
    coef_share.wait()

    def scaled(h, scale):
        column = jnp.transpose(jnp.broadcast_to(scale[0:1, :], (half, half)))[:, 0:1]
        scaled_out[h] = coef_all[h] * column

    scaled(core, scale_own[...])
    scaled(1 - core, scale_in[...])
    coef_out[...] = coef_all[...]

    def total_copy(k):
        index = lax.rem(me + k + 1, n)
        return pltpu.make_async_copy(other.at[at(index)], total_out.at[at(index)], total_sem.at[k])

    @pl.loop(0, n)
    def _(k):
        index = lax.rem(me + k + 1, n)
        load_momentum(index, k).wait()
        grad_copy(k).wait()
        other[at(index), :] = share[at(index), :] + (grad[at(index), :] + other[at(index), :])
        total_copy(k).start()

    @pl.loop(0, n)
    def _(k):
        total_copy(k).wait()


def split(value):
    high = value.astype(jnp.bfloat16)
    return high, (value - high.astype(jnp.float32)).astype(jnp.bfloat16)


def finish(step_scale, left, coefficients, scaled, total, weight, weight_out, momentum_out, coef_parts, scaled_parts):
    @pl.when(pl.program_id(0) == 0)
    def _():
        for source, parts in ((coefficients, coef_parts), (scaled, scaled_parts)):
            high, low = split(source[...])
            parts[...] = jnp.concatenate([high, low, high], axis=0)

    high, low = split(left[...])
    lefts = jnp.concatenate([high, high, low], axis=1)
    momentum_out[...] = total[...] - drop_share * jnp.dot(lefts, coef_parts[...], preferred_element_type=jnp.float32)
    weight_out[...] = weight[...] - step_scale * jnp.dot(lefts, scaled_parts[...], preferred_element_type=jnp.float32)


def update(step_scale, left, coefficients, scaled, total, weight):
    rows, cols = weight.shape
    rank = coefficients.shape[0]
    tile = math.gcd(rows, 128)
    wide = pl.BlockSpec((tile, cols), lambda i: (i, 0))
    whole = pl.BlockSpec((rank, cols), lambda i: (0, 0))
    return pl.pallas_call(
        functools.partial(finish, step_scale),
        grid=(rows // tile,),
        out_shape=(jax.ShapeDtypeStruct(weight.shape, weight.dtype),) * 2,
        in_specs=[pl.BlockSpec((tile, rank), lambda i: (i, 0)), whole, whole, wide, wide],
        out_specs=(wide, wide),
        scratch_shapes=[pltpu.VMEM((3 * rank, cols), jnp.bfloat16)] * 2,
        compiler_params=pltpu.CompilerParams(vmem_limit_bytes=60 * 1024 * 1024),
        cost_estimate=pl.CostEstimate(
            flops=12 * rows * cols * rank, bytes_accessed=18 * rows * cols, transcendentals=0
        ),
    )(left, coefficients, scaled, total, weight)


def exchange(n, momentum, right_basis, gradient):
    rows, cols = momentum.shape
    half = right_basis.shape[0]
    rank = 2 * half
    piece, lines = rows // n, rank // n
    f32 = jnp.float32
    vmem = pltpu.VMEM
    dma = pltpu.SemaphoreType.DMA
    any_spec = pl.BlockSpec(memory_space=pl.ANY)
    vmem_spec = pl.BlockSpec(memory_space=pltpu.VMEM)
    return pl.pallas_call(
        functools.partial(kernel, n),
        out_shape=(
            jax.ShapeDtypeStruct((rows, cols), f32),
            jax.ShapeDtypeStruct((rows, rank), f32),
            jax.ShapeDtypeStruct((2, half, cols), f32),
            jax.ShapeDtypeStruct((2, half, cols), f32),
        ),
        in_specs=[any_spec] * 3,
        out_specs=(any_spec, vmem_spec, vmem_spec, vmem_spec),
        scratch_shapes=[
            vmem((rows, cols), gradient.dtype),
            vmem((rows, cols), f32),
            vmem((rows, cols), f32),
            vmem((rows, cols), f32),
            vmem((2, half, cols), f32),
            vmem((n, piece, rank), f32),
            vmem((n, piece, rank), f32),
            vmem((piece, rank), f32),
            vmem((piece, rank), f32),
            vmem((rows, rank), f32),
            vmem((n, lines, rank), f32),
            vmem((n, lines, rank), f32),
            vmem((lines, rank), f32),
            vmem((lines, rank), f32),
            vmem((n, lines, rank), f32),
            vmem((rank, 2 * rank), f32),
            vmem((2, rows, half), f32),
            vmem((2, half, cols), f32),
            vmem((half, cols), f32),
            vmem((half, cols), f32),
            vmem((half, cols), f32),
            vmem((2, half, cols), f32),
            vmem((8, half), f32),
            vmem((n, 8, half), f32),
            vmem((8, half), f32),
            vmem((8, half), f32),
            dma((2, n)), dma((n,)), dma((n,)), dma((7,)), dma((7,)),
            dma((n,)), dma((n,)), dma((n,)), dma((n,)), dma((n,)), dma((n,)),
            dma((n,)), dma((n,)), dma((n,)), dma((n,)), dma((n,)), dma,
        ],
        compiler_params=pltpu.CompilerParams(
            collective_id=0, has_side_effects=True, vmem_limit_bytes=56 * 1024 * 1024
        ),
        cost_estimate=pl.CostEstimate(
            flops=6 * rows * cols * rank, bytes_accessed=20 * rows * cols, transcendentals=0
        ),
    )(momentum, right_basis, gradient)


def shards(n, step_scale, weight, momentum, right_basis, gradients):
    half, cols = right_basis.shape
    total, left_basis, coefficients, scaled = exchange(n, momentum, right_basis, gradients[0, 0])
    flat = scaled.reshape(2 * half, cols)
    weight, momentum = update(
        step_scale, left_basis, coefficients.reshape(2 * half, cols), flat, total, weight
    )
    first_rank = lax.axis_index("fsdp") * half
    return weight, momentum, lax.dynamic_slice_in_dim(flat, first_rank, half, 0)


def solution(mesh):
    assert mesh.shape["dp"] == 2 and mesh.shape["fsdp"] == 2
    n = mesh.shape["tensor"]

    def step(weight, momentum, right_basis, gradients):
        rows, width = weight.shape
        step_scale = step_size * math.sqrt(rows * width / right_basis.shape[0])
        return jax.shard_map(
            functools.partial(shards, n, step_scale),
            mesh=mesh,
            in_specs=(
                P("fsdp", "tensor"),
                P("fsdp", "tensor"),
                P("fsdp", "tensor"),
                P(None, "dp", "fsdp", "tensor"),
            ),
            out_specs=(P("fsdp", "tensor"), P("fsdp", "tensor"), P("fsdp", "tensor")),
            check_vma=False,
        )(weight, momentum, right_basis, gradients)

    return step
```

```python
import functools
import math

import jax
import jax.numpy as jnp
from jax import lax
from jax.experimental import pallas as pl
from jax.experimental.pallas import tpu as pltpu
from jax.sharding import PartitionSpec as P

highest = lax.Precision.HIGHEST
step_size = 0.3
drop_share = 0.05
guard_term = 1e-06
MESH = pl.DeviceIdType.MESH
PANEL = 32


def contract(left, right, left_dim, right_dim):
    return lax.dot_general(
        left,
        right,
        (((left_dim,), (right_dim,)), ((), ())),
        precision=highest,
        preferred_element_type=jnp.float32,
    )


def factor(aug):
    rank = aug.shape[0]

    @pl.loop(0, rank // PANEL)
    def _(block):
        first = pl.multiple_of(block * PANEL, PANEL)
        row = lax.broadcasted_iota(jnp.int32, (PANEL, 1), 0)
        lane = lax.broadcasted_iota(jnp.int32, (PANEL, rank), 1)

        def eliminate(step, work):
            column = jnp.sum(jnp.where(lane == first + step, work[:, :rank], 0.0), axis=1, keepdims=True)
            pivot = jnp.sum(jnp.where(row == step, column, 0.0), axis=0, keepdims=True)
            root = lax.rsqrt(pivot)
            line = jnp.sum(jnp.where(row == step, work, 0.0), axis=0, keepdims=True) * root
            rest = work - jnp.where(row > step, column * root, 0.0) * line
            return jnp.where(row == step, line, rest)

        work = lax.fori_loop(0, PANEL, eliminate, aug[pl.ds(first, PANEL), :])
        aug[pl.ds(first, PANEL), :] = work
        below = jnp.where(lane >= first + PANEL, work[:, :rank], 0.0)
        aug[...] -= contract(below, work, 0, 0)


def kernel(
    n, momentum, right_basis, gradients, total_out, left_out, coef_out, scaled_out,
    grad_in, share, grad, other, basis, part, part_in, own, own_in, sketch,
    gram_part, gram_in, gram_sum, gram_pair, gram_all, aug, left,
    coef_part, coef_in, coef_sum, coef_pair, coef_all, norm_own, norm_in, scale_own, scale_in,
    load_sem, grad_send, grad_recv, pair_send, pair_recv,
    part_send, part_recv, row_send, row_recv, gram_send, gram_recv,
    gall_send, gall_recv, norm_send, norm_recv, total_sem, base_sem,
):
    dp, core, me = lax.axis_index("dp"), lax.axis_index("fsdp"), lax.axis_index("tensor")
    rows, _ = share.shape
    piece = rows // n
    half = right_basis.shape[0]
    rank = 2 * half
    lines = rank // n

    def at(index):
        return pl.ds(pl.multiple_of(index * piece, piece), piece)

    def load_momentum(index, slot):
        return pltpu.make_async_copy(momentum.at[at(index)], share.at[at(index)], load_sem.at[1, slot])

    def load(index, slot):
        return (
            pltpu.make_async_copy(gradients.at[at(index)], grad_in.at[at(index)], load_sem.at[0, slot]),
            load_momentum(index, slot),
        )

    base = pltpu.make_async_copy(right_basis, basis.at[core], base_sem)
    base.start()

    @pl.loop(0, n)
    def _(k):
        for copy in load(lax.rem(me + k + 1, n), k):
            copy.start()

    barrier = pltpu.get_barrier_semaphore()
    pl.semaphore_signal(barrier, inc=1, device_id={"dp": 1 - dp}, device_id_type=MESH)
    pl.semaphore_signal(barrier, inc=1, device_id={"fsdp": 1 - core}, device_id_type=MESH)

    @pl.loop(1, n)
    def _(k):
        pl.semaphore_signal(barrier, inc=1, device_id={"tensor": lax.rem(me + k, n)}, device_id_type=MESH)

    pl.semaphore_wait(barrier, n + 1)

    def remote(src, dst, send, recv, where):
        return pltpu.make_async_remote_copy(
            src_ref=src, dst_ref=dst, send_sem=send, recv_sem=recv, device_id=where, device_id_type=MESH
        )

    def pair(index, src, dst, axis):
        where = {axis: 1 - (dp if axis == "dp" else core)}
        return remote(src, dst, pair_send.at[index], pair_recv.at[index], where)

    def grad_copy(k):
        index = lax.rem(me + k + 1, n)
        return remote(grad.at[at(index)], other.at[at(index)], grad_send.at[k], grad_recv.at[k], {"dp": 1 - dp})

    def send_grads(begin, end):
        @pl.loop(begin, end)
        def _(k):
            grad_copy(k).start()

    base.wait()
    basis_copy = pair(0, basis.at[core], basis.at[core], "fsdp")
    basis_copy.start()
    stages = [n * i // 8 for i in (3, 5, 6, 7, 8)]

    @pl.loop(0, n)
    def _(k):
        index = lax.rem(me + k + 1, n)
        for copy in load(index, k):
            copy.wait()
        value = grad_in[at(index), :].astype(jnp.float32)
        grad[at(index), :] = value
        share[at(index), :] = share[at(index), :] * 0.5 + value

        @pl.when(k < stages[0])
        def _():
            grad_copy(k).start()

    basis_copy.wait()

    def part_copy(k):
        return remote(
            part.at[lax.rem(me + k, n)], part_in.at[k], part_send.at[k], part_recv.at[k],
            {"tensor": lax.rem(me + k, n)},
        )

    @pl.loop(1, n + 1)
    def _(k):
        index = lax.rem(me + k, n)
        value = share[at(index), :]
        for h in range(2):
            part[index, :, h * half : (h + 1) * half] = contract(value, basis[h], 1, 1)

        @pl.when(k < n)
        def _():
            part_copy(k).start()

    own[...] = part[me]

    @pl.loop(1, n)
    def _(k):
        part_copy(k).wait()
        own[...] += part_in[k]

    dp_copy = pair(1, own, own_in, "dp")
    dp_copy.start()
    send_grads(stages[0], stages[1])
    dp_copy.wait()
    sketch[at(me), :] = own[...] + own_in[...]

    block = sketch[at(me), :]
    gram = contract(block, block, 0, 0)
    for i in range(n):
        gram_part[i] = gram[i * lines : (i + 1) * lines, :]

    def gram_copy(k):
        return remote(
            gram_part.at[lax.rem(me + k, n)], gram_in.at[k], gram_send.at[k], gram_recv.at[k],
            {"tensor": lax.rem(me + k, n)},
        )

    @pl.loop(1, n)
    def _(k):
        gram_copy(k).start()

    gram_sum[...] = gram_part[me]

    @pl.loop(1, n)
    def _(k):
        gram_copy(k).wait()
        gram_sum[...] += gram_in[k]

    gram_swap = pair(2, gram_sum, gram_pair, "fsdp")
    gram_swap.start()
    gram_swap.wait()
    gram_all[me] = gram_sum[...] + gram_pair[...]

    def gall_copy(k):
        return remote(
            gram_all.at[me], gram_all.at[me], gall_send.at[k], gall_recv.at[k], {"tensor": lax.rem(me + k, n)}
        )

    def row_copy(k):
        return remote(
            sketch.at[at(me)], sketch.at[at(me)], row_send.at[k], row_recv.at[k], {"tensor": lax.rem(me + k, n)}
        )

    def gall_arrival(k):
        source = lax.rem(me + n - k, n)
        return remote(
            gram_all.at[source], gram_all.at[source], gall_send.at[k], gall_recv.at[k],
            {"tensor": lax.rem(me + k, n)},
        )

    def row_arrival(k):
        source = lax.rem(me + n - k, n)
        return remote(
            sketch.at[at(source)], sketch.at[at(source)], row_send.at[k], row_recv.at[k],
            {"tensor": lax.rem(me + k, n)},
        )

    @pl.loop(1, n)
    def _(k):
        gall_copy(k).start()

    @pl.loop(1, n)
    def _(k):
        row_copy(k).start()

    send_grads(stages[1], stages[2])

    @pl.loop(1, n)
    def _(k):
        gall_copy(k).wait_send()
        gall_arrival(k).wait_recv()

    for i in range(n):
        aug[i * lines : (i + 1) * lines, :rank] = gram_all[i]
    diagonal = lax.broadcasted_iota(jnp.int32, (rank, rank), 0) == lax.broadcasted_iota(jnp.int32, (rank, rank), 1)
    aug[:, rank:] = jnp.where(diagonal, 1.0, 0.0)
    factor(aug)
    send_grads(stages[2], stages[3])

    @pl.loop(1, n)
    def _(k):
        row_copy(k).wait_send()
        row_arrival(k).wait_recv()

    coef_part[...] = jnp.zeros_like(coef_part)

    @pl.loop(0, n)
    def _(k):
        block = sketch[at(k), :]
        for h in range(2):
            value = contract(block, aug[h * half : (h + 1) * half, rank:], 1, 1)
            left[h, at(k), :] = value
            left_out[at(k), h * half : (h + 1) * half] = value

    def accumulate(h):
        @pl.loop(0, n)
        def _(k):
            coef_part[h] += contract(left[h, at(k), :], share[at(k), :], 0, 0)

    accumulate(1 - core)
    coef_swap = pair(3, coef_part.at[1 - core], coef_in, "fsdp")
    coef_swap.start()
    accumulate(core)

    @pl.loop(0, n)
    def _(k):
        load_momentum(lax.rem(me + k + 1, n), k).start()

    coef_swap.wait()
    coef_sum[...] = coef_part[core] + coef_in[...]
    coef_dp = pair(4, coef_sum, coef_pair, "dp")
    coef_dp.start()
    send_grads(stages[3], stages[4])
    coef_dp.wait()
    coef_all[core] = coef_sum[...] + coef_pair[...]
    coef_share = pair(5, coef_all.at[core], coef_all.at[core], "fsdp")
    coef_share.start()

    value = coef_all[core]
    norm_own[...] = contract(jnp.ones((8, value.shape[1]), jnp.float32), value * value, 1, 1)

    def norm_copy(k):
        return remote(
            norm_own, norm_in.at[me], norm_send.at[k], norm_recv.at[k], {"tensor": lax.rem(me + k, n)}
        )

    def norm_arrival(k):
        source = lax.rem(me + n - k, n)
        return remote(
            norm_own, norm_in.at[source], norm_send.at[k], norm_recv.at[k], {"tensor": lax.rem(me + k, n)}
        )

    @pl.loop(1, n)
    def _(k):
        norm_copy(k).start()

    norm_in[me] = norm_own[...]

    @pl.loop(1, n)
    def _(k):
        norm_copy(k).wait_send()
        norm_arrival(k).wait_recv()

    total = norm_in[0]
    for i in range(1, n):
        total = total + norm_in[i]
    scale_own[...] = lax.rsqrt(total + guard_term)
    scale_copy = pair(6, scale_own, scale_in, "fsdp")
    scale_copy.start()
    scale_copy.wait()
    coef_share.wait()

    def scaled(h, scale):
        column = jnp.transpose(jnp.broadcast_to(scale[0:1, :], (half, half)))[:, 0:1]
        scaled_out[h] = coef_all[h] * column

    scaled(core, scale_own[...])
    scaled(1 - core, scale_in[...])
    coef_out[...] = coef_all[...]

    def total_copy(k):
        index = lax.rem(me + k + 1, n)
        return pltpu.make_async_copy(other.at[at(index)], total_out.at[at(index)], total_sem.at[k])

    @pl.loop(0, n)
    def _(k):
        index = lax.rem(me + k + 1, n)
        load_momentum(index, k).wait()
        grad_copy(k).wait()
        other[at(index), :] = share[at(index), :] + (grad[at(index), :] + other[at(index), :])
        total_copy(k).start()

    @pl.loop(0, n)
    def _(k):
        total_copy(k).wait()


def split(value):
    high = value.astype(jnp.bfloat16)
    return high, (value - high.astype(jnp.float32)).astype(jnp.bfloat16)


def finish(step_scale, left, coefficients, scaled, total, weight, weight_out, momentum_out, coef_parts, scaled_parts):
    @pl.when(pl.program_id(0) == 0)
    def _():
        for source, parts in ((coefficients, coef_parts), (scaled, scaled_parts)):
            high, low = split(source[...])
            parts[...] = jnp.concatenate([high, low, high], axis=0)

    high, low = split(left[...])
    lefts = jnp.concatenate([high, high, low], axis=1)
    momentum_out[...] = total[...] - drop_share * jnp.dot(lefts, coef_parts[...], preferred_element_type=jnp.float32)
    weight_out[...] = weight[...] - step_scale * jnp.dot(lefts, scaled_parts[...], preferred_element_type=jnp.float32)


def update(step_scale, left, coefficients, scaled, total, weight):
    rows, cols = weight.shape
    rank = coefficients.shape[0]
    tile = math.gcd(rows, 256)
    wide = pl.BlockSpec((tile, cols), lambda i: (i, 0))
    whole = pl.BlockSpec((rank, cols), lambda i: (0, 0))
    return pl.pallas_call(
        functools.partial(finish, step_scale),
        grid=(rows // tile,),
        out_shape=(jax.ShapeDtypeStruct(weight.shape, weight.dtype),) * 2,
        in_specs=[pl.BlockSpec((tile, rank), lambda i: (i, 0)), whole, whole, wide, wide],
        out_specs=(wide, wide),
        scratch_shapes=[pltpu.VMEM((3 * rank, cols), jnp.bfloat16)] * 2,
        compiler_params=pltpu.CompilerParams(vmem_limit_bytes=60 * 1024 * 1024),
        cost_estimate=pl.CostEstimate(
            flops=12 * rows * cols * rank, bytes_accessed=18 * rows * cols, transcendentals=0
        ),
    )(left, coefficients, scaled, total, weight)


def exchange(n, momentum, right_basis, gradient):
    rows, cols = momentum.shape
    half = right_basis.shape[0]
    rank = 2 * half
    piece, lines = rows // n, rank // n
    f32 = jnp.float32
    vmem = pltpu.VMEM
    dma = pltpu.SemaphoreType.DMA
    any_spec = pl.BlockSpec(memory_space=pl.ANY)
    vmem_spec = pl.BlockSpec(memory_space=pltpu.VMEM)
    return pl.pallas_call(
        functools.partial(kernel, n),
        out_shape=(
            jax.ShapeDtypeStruct((rows, cols), f32),
            jax.ShapeDtypeStruct((rows, rank), f32),
            jax.ShapeDtypeStruct((2, half, cols), f32),
            jax.ShapeDtypeStruct((2, half, cols), f32),
        ),
        in_specs=[any_spec] * 3,
        out_specs=(any_spec, vmem_spec, vmem_spec, vmem_spec),
        scratch_shapes=[
            vmem((rows, cols), gradient.dtype),
            vmem((rows, cols), f32),
            vmem((rows, cols), f32),
            vmem((rows, cols), f32),
            vmem((2, half, cols), f32),
            vmem((n, piece, rank), f32),
            vmem((n, piece, rank), f32),
            vmem((piece, rank), f32),
            vmem((piece, rank), f32),
            vmem((rows, rank), f32),
            vmem((n, lines, rank), f32),
            vmem((n, lines, rank), f32),
            vmem((lines, rank), f32),
            vmem((lines, rank), f32),
            vmem((n, lines, rank), f32),
            vmem((rank, 2 * rank), f32),
            vmem((2, rows, half), f32),
            vmem((2, half, cols), f32),
            vmem((half, cols), f32),
            vmem((half, cols), f32),
            vmem((half, cols), f32),
            vmem((2, half, cols), f32),
            vmem((8, half), f32),
            vmem((n, 8, half), f32),
            vmem((8, half), f32),
            vmem((8, half), f32),
            dma((2, n)), dma((n,)), dma((n,)), dma((7,)), dma((7,)),
            dma((n,)), dma((n,)), dma((n,)), dma((n,)), dma((n,)), dma((n,)),
            dma((n,)), dma((n,)), dma((n,)), dma((n,)), dma((n,)), dma,
        ],
        compiler_params=pltpu.CompilerParams(
            collective_id=0, has_side_effects=True, vmem_limit_bytes=56 * 1024 * 1024
        ),
        cost_estimate=pl.CostEstimate(
            flops=6 * rows * cols * rank, bytes_accessed=20 * rows * cols, transcendentals=0
        ),
    )(momentum, right_basis, gradient)


def shards(n, step_scale, weight, momentum, right_basis, gradients):
    half, cols = right_basis.shape
    total, left_basis, coefficients, scaled = exchange(n, momentum, right_basis, gradients[0, 0])
    flat = scaled.reshape(2 * half, cols)
    weight, momentum = update(
        step_scale, left_basis, coefficients.reshape(2 * half, cols), flat, total, weight
    )
    first_rank = lax.axis_index("fsdp") * half
    return weight, momentum, lax.dynamic_slice_in_dim(flat, first_rank, half, 0)


def solution(mesh):
    assert mesh.shape["dp"] == 2 and mesh.shape["fsdp"] == 2
    n = mesh.shape["tensor"]

    def step(weight, momentum, right_basis, gradients):
        rows, width = weight.shape
        step_scale = step_size * math.sqrt(rows * width / right_basis.shape[0])
        return jax.shard_map(
            functools.partial(shards, n, step_scale),
            mesh=mesh,
            in_specs=(
                P("fsdp", "tensor"),
                P("fsdp", "tensor"),
                P("fsdp", "tensor"),
                P(None, "dp", "fsdp", "tensor"),
            ),
            out_specs=(P("fsdp", "tensor"), P("fsdp", "tensor"), P("fsdp", "tensor")),
            check_vma=False,
        )(weight, momentum, right_basis, gradients)

    return step
```

```python
import functools
import math

import jax
import jax.numpy as jnp
from jax import lax
from jax.experimental import pallas as pl
from jax.experimental.pallas import tpu as pltpu
from jax.sharding import PartitionSpec as P

highest = lax.Precision.HIGHEST
step_size = 0.3
drop_share = 0.05
guard_term = 1e-06
MESH = pl.DeviceIdType.MESH
PANEL = 32


def contract(left, right, left_dim, right_dim):
    return lax.dot_general(
        left,
        right,
        (((left_dim,), (right_dim,)), ((), ())),
        precision=highest,
        preferred_element_type=jnp.float32,
    )


def factor(aug):
    rank = aug.shape[0]

    @pl.loop(0, rank // PANEL)
    def _(block):
        first = pl.multiple_of(block * PANEL, PANEL)
        row = lax.broadcasted_iota(jnp.int32, (PANEL, 1), 0)
        lane = lax.broadcasted_iota(jnp.int32, (PANEL, rank), 1)

        def eliminate(step, work):
            column = jnp.sum(jnp.where(lane == first + step, work[:, :rank], 0.0), axis=1, keepdims=True)
            pivot = jnp.sum(jnp.where(row == step, column, 0.0), axis=0, keepdims=True)
            root = lax.rsqrt(pivot)
            line = jnp.sum(jnp.where(row == step, work, 0.0), axis=0, keepdims=True) * root
            rest = work - jnp.where(row > step, column * root, 0.0) * line
            return jnp.where(row == step, line, rest)

        work = lax.fori_loop(0, PANEL, eliminate, aug[pl.ds(first, PANEL), :])
        aug[pl.ds(first, PANEL), :] = work
        below = jnp.where(lane >= first + PANEL, work[:, :rank], 0.0)
        aug[...] -= contract(below, work, 0, 0)


def kernel(
    n, momentum, right_basis, gradients, total_out, left_out, coef_out, scaled_out,
    grad_in, share, grad, other, basis, part, part_in, own, own_in, sketch,
    gram_part, gram_in, gram_sum, gram_pair, gram_all, aug, left,
    coef_part, coef_in, coef_sum, coef_pair, coef_all, norm_own, norm_in, scale_own, scale_in,
    load_sem, grad_send, grad_recv, pair_send, pair_recv,
    part_send, part_recv, row_send, row_recv, gram_send, gram_recv,
    gall_send, gall_recv, norm_send, norm_recv, total_sem, base_sem,
):
    dp, core, me = lax.axis_index("dp"), lax.axis_index("fsdp"), lax.axis_index("tensor")
    rows, _ = share.shape
    piece = rows // n
    half = right_basis.shape[0]
    rank = 2 * half
    lines = rank // n

    def at(index):
        return pl.ds(pl.multiple_of(index * piece, piece), piece)

    def load_momentum(index, slot):
        return pltpu.make_async_copy(momentum.at[at(index)], share.at[at(index)], load_sem.at[1, slot])

    def load(index, slot):
        return (
            pltpu.make_async_copy(gradients.at[at(index)], grad_in.at[at(index)], load_sem.at[0, slot]),
            load_momentum(index, slot),
        )

    base = pltpu.make_async_copy(right_basis, basis.at[core], base_sem)
    base.start()

    @pl.loop(0, n)
    def _(k):
        for copy in load(lax.rem(me + k + 1, n), k):
            copy.start()

    barrier = pltpu.get_barrier_semaphore()
    pl.semaphore_signal(barrier, inc=1, device_id={"dp": 1 - dp}, device_id_type=MESH)
    pl.semaphore_signal(barrier, inc=1, device_id={"fsdp": 1 - core}, device_id_type=MESH)

    @pl.loop(1, n)
    def _(k):
        pl.semaphore_signal(barrier, inc=1, device_id={"tensor": lax.rem(me + k, n)}, device_id_type=MESH)

    pl.semaphore_wait(barrier, n + 1)

    def remote(src, dst, send, recv, where):
        return pltpu.make_async_remote_copy(
            src_ref=src, dst_ref=dst, send_sem=send, recv_sem=recv, device_id=where, device_id_type=MESH
        )

    def pair(index, src, dst, axis):
        where = {axis: 1 - (dp if axis == "dp" else core)}
        return remote(src, dst, pair_send.at[index], pair_recv.at[index], where)

    def grad_copy(k):
        index = lax.rem(me + k + 1, n)
        return remote(grad.at[at(index)], other.at[at(index)], grad_send.at[k], grad_recv.at[k], {"dp": 1 - dp})

    def send_grads(begin, end):
        @pl.loop(begin, end)
        def _(k):
            grad_copy(k).start()

    base.wait()
    basis_copy = pair(0, basis.at[core], basis.at[core], "fsdp")
    basis_copy.start()
    stages = [n * i // 8 for i in (3, 5, 7, 7, 8)]

    @pl.loop(0, n)
    def _(k):
        index = lax.rem(me + k + 1, n)
        for copy in load(index, k):
            copy.wait()
        value = grad_in[at(index), :].astype(jnp.float32)
        grad[at(index), :] = value
        share[at(index), :] = share[at(index), :] * 0.5 + value

        @pl.when(k < stages[0])
        def _():
            grad_copy(k).start()

    basis_copy.wait()

    def part_copy(k):
        return remote(
            part.at[lax.rem(me + k, n)], part_in.at[k], part_send.at[k], part_recv.at[k],
            {"tensor": lax.rem(me + k, n)},
        )

    @pl.loop(1, n + 1)
    def _(k):
        index = lax.rem(me + k, n)
        value = share[at(index), :]
        for h in range(2):
            part[index, :, h * half : (h + 1) * half] = contract(value, basis[h], 1, 1)

        @pl.when(k < n)
        def _():
            part_copy(k).start()

    own[...] = part[me]

    @pl.loop(1, n)
    def _(k):
        part_copy(k).wait()
        own[...] += part_in[k]

    dp_copy = pair(1, own, own_in, "dp")
    dp_copy.start()
    send_grads(stages[0], stages[1])
    dp_copy.wait()
    sketch[at(me), :] = own[...] + own_in[...]

    block = sketch[at(me), :]
    gram = contract(block, block, 0, 0)
    for i in range(n):
        gram_part[i] = gram[i * lines : (i + 1) * lines, :]

    def gram_copy(k):
        return remote(
            gram_part.at[lax.rem(me + k, n)], gram_in.at[k], gram_send.at[k], gram_recv.at[k],
            {"tensor": lax.rem(me + k, n)},
        )

    @pl.loop(1, n)
    def _(k):
        gram_copy(k).start()

    gram_sum[...] = gram_part[me]

    @pl.loop(1, n)
    def _(k):
        gram_copy(k).wait()
        gram_sum[...] += gram_in[k]

    gram_swap = pair(2, gram_sum, gram_pair, "fsdp")
    gram_swap.start()
    gram_swap.wait()
    gram_all[me] = gram_sum[...] + gram_pair[...]

    def gall_copy(k):
        return remote(
            gram_all.at[me], gram_all.at[me], gall_send.at[k], gall_recv.at[k], {"tensor": lax.rem(me + k, n)}
        )

    def row_copy(k):
        return remote(
            sketch.at[at(me)], sketch.at[at(me)], row_send.at[k], row_recv.at[k], {"tensor": lax.rem(me + k, n)}
        )

    def gall_arrival(k):
        source = lax.rem(me + n - k, n)
        return remote(
            gram_all.at[source], gram_all.at[source], gall_send.at[k], gall_recv.at[k],
            {"tensor": lax.rem(me + k, n)},
        )

    def row_arrival(k):
        source = lax.rem(me + n - k, n)
        return remote(
            sketch.at[at(source)], sketch.at[at(source)], row_send.at[k], row_recv.at[k],
            {"tensor": lax.rem(me + k, n)},
        )

    @pl.loop(1, n)
    def _(k):
        gall_copy(k).start()

    @pl.loop(1, n)
    def _(k):
        row_copy(k).start()

    send_grads(stages[1], stages[2])

    @pl.loop(1, n)
    def _(k):
        gall_copy(k).wait_send()
        gall_arrival(k).wait_recv()

    for i in range(n):
        aug[i * lines : (i + 1) * lines, :rank] = gram_all[i]
    diagonal = lax.broadcasted_iota(jnp.int32, (rank, rank), 0) == lax.broadcasted_iota(jnp.int32, (rank, rank), 1)
    aug[:, rank:] = jnp.where(diagonal, 1.0, 0.0)
    factor(aug)
    send_grads(stages[2], stages[3])

    @pl.loop(1, n)
    def _(k):
        row_copy(k).wait_send()
        row_arrival(k).wait_recv()

    coef_part[...] = jnp.zeros_like(coef_part)

    @pl.loop(0, n)
    def _(k):
        block = sketch[at(k), :]
        for h in range(2):
            value = contract(block, aug[h * half : (h + 1) * half, rank:], 1, 1)
            left[h, at(k), :] = value
            left_out[at(k), h * half : (h + 1) * half] = value

    def accumulate(h):
        @pl.loop(0, n)
        def _(k):
            coef_part[h] += contract(left[h, at(k), :], share[at(k), :], 0, 0)

    accumulate(1 - core)
    coef_swap = pair(3, coef_part.at[1 - core], coef_in, "fsdp")
    coef_swap.start()
    accumulate(core)

    @pl.loop(0, n)
    def _(k):
        load_momentum(lax.rem(me + k + 1, n), k).start()

    coef_swap.wait()
    coef_sum[...] = coef_part[core] + coef_in[...]
    coef_dp = pair(4, coef_sum, coef_pair, "dp")
    coef_dp.start()
    send_grads(stages[3], stages[4])
    coef_dp.wait()
    coef_all[core] = coef_sum[...] + coef_pair[...]
    coef_share = pair(5, coef_all.at[core], coef_all.at[core], "fsdp")
    coef_share.start()

    value = coef_all[core]
    norm_own[...] = contract(jnp.ones((8, value.shape[1]), jnp.float32), value * value, 1, 1)

    def norm_copy(k):
        return remote(
            norm_own, norm_in.at[me], norm_send.at[k], norm_recv.at[k], {"tensor": lax.rem(me + k, n)}
        )

    def norm_arrival(k):
        source = lax.rem(me + n - k, n)
        return remote(
            norm_own, norm_in.at[source], norm_send.at[k], norm_recv.at[k], {"tensor": lax.rem(me + k, n)}
        )

    @pl.loop(1, n)
    def _(k):
        norm_copy(k).start()

    norm_in[me] = norm_own[...]

    @pl.loop(1, n)
    def _(k):
        norm_copy(k).wait_send()
        norm_arrival(k).wait_recv()

    total = norm_in[0]
    for i in range(1, n):
        total = total + norm_in[i]
    scale_own[...] = lax.rsqrt(total + guard_term)
    scale_copy = pair(6, scale_own, scale_in, "fsdp")
    scale_copy.start()
    scale_copy.wait()
    coef_share.wait()

    def scaled(h, scale):
        column = jnp.transpose(jnp.broadcast_to(scale[0:1, :], (half, half)))[:, 0:1]
        scaled_out[h] = coef_all[h] * column

    scaled(core, scale_own[...])
    scaled(1 - core, scale_in[...])
    coef_out[...] = coef_all[...]

    def total_copy(k):
        index = lax.rem(me + k + 1, n)
        return pltpu.make_async_copy(other.at[at(index)], total_out.at[at(index)], total_sem.at[k])

    @pl.loop(0, n)
    def _(k):
        index = lax.rem(me + k + 1, n)
        load_momentum(index, k).wait()
        grad_copy(k).wait()
        other[at(index), :] = share[at(index), :] + (grad[at(index), :] + other[at(index), :])
        total_copy(k).start()

    @pl.loop(0, n)
    def _(k):
        total_copy(k).wait()


def split(value):
    high = value.astype(jnp.bfloat16)
    return high, (value - high.astype(jnp.float32)).astype(jnp.bfloat16)


def finish(step_scale, left, coefficients, scaled, total, weight, weight_out, momentum_out, coef_parts, scaled_parts):
    @pl.when(pl.program_id(0) == 0)
    def _():
        for source, parts in ((coefficients, coef_parts), (scaled, scaled_parts)):
            high, low = split(source[...])
            parts[...] = jnp.concatenate([high, low, high], axis=0)

    high, low = split(left[...])
    lefts = jnp.concatenate([high, high, low], axis=1)
    momentum_out[...] = total[...] - drop_share * jnp.dot(lefts, coef_parts[...], preferred_element_type=jnp.float32)
    weight_out[...] = weight[...] - step_scale * jnp.dot(lefts, scaled_parts[...], preferred_element_type=jnp.float32)


def update(step_scale, left, coefficients, scaled, total, weight):
    rows, cols = weight.shape
    rank = coefficients.shape[0]
    tile = math.gcd(rows, 512)
    wide = pl.BlockSpec((tile, cols), lambda i: (i, 0))
    whole = pl.BlockSpec((rank, cols), lambda i: (0, 0))
    return pl.pallas_call(
        functools.partial(finish, step_scale),
        grid=(rows // tile,),
        out_shape=(jax.ShapeDtypeStruct(weight.shape, weight.dtype),) * 2,
        in_specs=[pl.BlockSpec((tile, rank), lambda i: (i, 0)), whole, whole, wide, wide],
        out_specs=(wide, wide),
        scratch_shapes=[pltpu.VMEM((3 * rank, cols), jnp.bfloat16)] * 2,
        compiler_params=pltpu.CompilerParams(vmem_limit_bytes=60 * 1024 * 1024),
        cost_estimate=pl.CostEstimate(
            flops=12 * rows * cols * rank, bytes_accessed=18 * rows * cols, transcendentals=0
        ),
    )(left, coefficients, scaled, total, weight)


def exchange(n, momentum, right_basis, gradient):
    rows, cols = momentum.shape
    half = right_basis.shape[0]
    rank = 2 * half
    piece, lines = rows // n, rank // n
    f32 = jnp.float32
    vmem = pltpu.VMEM
    dma = pltpu.SemaphoreType.DMA
    any_spec = pl.BlockSpec(memory_space=pl.ANY)
    vmem_spec = pl.BlockSpec(memory_space=pltpu.VMEM)
    return pl.pallas_call(
        functools.partial(kernel, n),
        out_shape=(
            jax.ShapeDtypeStruct((rows, cols), f32),
            jax.ShapeDtypeStruct((rows, rank), f32),
            jax.ShapeDtypeStruct((2, half, cols), f32),
            jax.ShapeDtypeStruct((2, half, cols), f32),
        ),
        in_specs=[any_spec] * 3,
        out_specs=(any_spec, vmem_spec, vmem_spec, vmem_spec),
        scratch_shapes=[
            vmem((rows, cols), gradient.dtype),
            vmem((rows, cols), f32),
            vmem((rows, cols), f32),
            vmem((rows, cols), f32),
            vmem((2, half, cols), f32),
            vmem((n, piece, rank), f32),
            vmem((n, piece, rank), f32),
            vmem((piece, rank), f32),
            vmem((piece, rank), f32),
            vmem((rows, rank), f32),
            vmem((n, lines, rank), f32),
            vmem((n, lines, rank), f32),
            vmem((lines, rank), f32),
            vmem((lines, rank), f32),
            vmem((n, lines, rank), f32),
            vmem((rank, 2 * rank), f32),
            vmem((2, rows, half), f32),
            vmem((2, half, cols), f32),
            vmem((half, cols), f32),
            vmem((half, cols), f32),
            vmem((half, cols), f32),
            vmem((2, half, cols), f32),
            vmem((8, half), f32),
            vmem((n, 8, half), f32),
            vmem((8, half), f32),
            vmem((8, half), f32),
            dma((2, n)), dma((n,)), dma((n,)), dma((7,)), dma((7,)),
            dma((n,)), dma((n,)), dma((n,)), dma((n,)), dma((n,)), dma((n,)),
            dma((n,)), dma((n,)), dma((n,)), dma((n,)), dma((n,)), dma,
        ],
        compiler_params=pltpu.CompilerParams(
            collective_id=0, has_side_effects=True, vmem_limit_bytes=56 * 1024 * 1024
        ),
        cost_estimate=pl.CostEstimate(
            flops=6 * rows * cols * rank, bytes_accessed=20 * rows * cols, transcendentals=0
        ),
    )(momentum, right_basis, gradient)


def shards(n, step_scale, weight, momentum, right_basis, gradients):
    half, cols = right_basis.shape
    total, left_basis, coefficients, scaled = exchange(n, momentum, right_basis, gradients[0, 0])
    flat = scaled.reshape(2 * half, cols)
    weight, momentum = update(
        step_scale, left_basis, coefficients.reshape(2 * half, cols), flat, total, weight
    )
    first_rank = lax.axis_index("fsdp") * half
    return weight, momentum, lax.dynamic_slice_in_dim(flat, first_rank, half, 0)


def solution(mesh):
    assert mesh.shape["dp"] == 2 and mesh.shape["fsdp"] == 2
    n = mesh.shape["tensor"]

    def step(weight, momentum, right_basis, gradients):
        rows, width = weight.shape
        step_scale = step_size * math.sqrt(rows * width / right_basis.shape[0])
        return jax.shard_map(
            functools.partial(shards, n, step_scale),
            mesh=mesh,
            in_specs=(
                P("fsdp", "tensor"),
                P("fsdp", "tensor"),
                P("fsdp", "tensor"),
                P(None, "dp", "fsdp", "tensor"),
            ),
            out_specs=(P("fsdp", "tensor"), P("fsdp", "tensor"), P("fsdp", "tensor")),
            check_vma=False,
        )(weight, momentum, right_basis, gradients)

    return step
```
